32 devices in a mesh: row: 4 (over x, core), col: 8 (over z, y).
Axes of the slice: x: 2, y: 2, z: 4, core: 2. Of those that a mesh axis runs over, the one named last changes fastest.
Arguments:
- a_blocks: float32 [96, 16, 128, 128], P('col', 'row'), may hold values from -0.25 to 0.25
- a_cols: int32 [96, 16], P('col'), may hold values from 0 to 15, as said below
- a_lengths: int32 [96], P('col'), may hold values from 1 to 16, as said below
- b_blocks: float32 [16, 4, 128, 128], P('col', 'row'), may hold values from -6 to 6
- b_cols: int32 [16, 4], P(None, 'row'), may hold values from 0 to 7
- c_cols: int32 [96, 16], P('col', 'row'), may hold values from 0 to 7, as said below
- order: int32 [16], replicated, may hold values from 0 to 15, each once
Outputs:
- c_blocks: float32 [96, 16, 128, 128], P('col', 'row')
The draws below stay inside these ranges and needn't reach their ends.
Inputs may be any that keep to these rules, and one draw needn't show every extreme that they name: `a_cols`: the 16 entries of one row are distinct. `a_lengths`: the first row has 16 live slots; slots at or after a row's length hold blocks that are not used. `c_cols`: the 4 entries of one row in one row group are distinct. `order`: each number once.
All inputs are finite; a program needn't handle non-finite values.
Results may differ from the reference program's by a relative error of at most 0.0003.
Values sent between devices are 32-bit elements; how exact they have to be, the bound alone decides.
A program may use at most 64 MiB of HBM per device.

```python
import jax
import jax.numpy as jnp
from jax import lax

BLOCK = 128
SLOTS = 16
ROWS_DEV = 12
WIN = 8
CSLOTS = 4
ROWS = 96
NACT = 16
C_ALL = 16
N_ROW = 4


def draw_a_cols(key, part):
    scores = jax.random.randint(key, (ROWS, NACT), 0, 65536) * NACT + jnp.arange(NACT, dtype=jnp.int32)[None, :]
    ranked = jnp.argsort(scores, axis=-1)
    return ranked[:, :SLOTS].astype(jnp.int32)


def draw_a_lengths(key, part):
    first_key = jax.random.fold_in(key, 11)
    second_key = jax.random.fold_in(key, 23)
    level_code = jax.random.randint(first_key, (ROWS // ROWS_DEV,), 0, 8)
    level = jnp.where(level_code == 7, 4, jnp.where(level_code == 6, 2, 1))
    level_rows = jnp.repeat(level, ROWS_DEV)
    jitter = jax.random.randint(second_key, (ROWS,), 0, SLOTS // 8 + 1)
    lengths = jnp.clip(level_rows * (SLOTS // 4) - jitter, 1, SLOTS)
    lengths = lengths.at[0].set(SLOTS)
    return lengths.astype(jnp.int32)


def draw_c_cols(key, part):
    group_count = C_ALL // CSLOTS
    scores = jax.random.randint(key, (ROWS, group_count, WIN), 0, 65536) * WIN + jnp.arange(WIN, dtype=jnp.int32)
    ranked = jnp.argsort(scores, axis=-1)
    return ranked[:, :, :CSLOTS].reshape(ROWS, C_ALL).astype(jnp.int32)


def touch_ends(values, key, low, largest):
    longest = values.shape.index(max(values.shape))
    spots = []
    for shift in (0, 1):
        where = [jax.random.randint(jax.random.fold_in(key, axis), (), 0, length) for axis, length in enumerate(values.shape)]
        where[longest] = (where[longest] + shift) % values.shape[longest]
        spots.append(tuple(where))
    return values.at[spots[0]].set(low).at[spots[1]].set(largest)


def block_scale(own_key, shape, shards, smallest, high):
    gain, own = 1.0, jax.random.fold_in(own_key, 6)
    for dim, blocks in shards:
        draws = jnp.exp(jax.random.uniform(jax.random.fold_in(own, dim), (blocks,), jnp.float32, smallest / len(shards), high / len(shards)))
        gain = gain * jnp.repeat(draws, shape[dim] // blocks).reshape([-1 if axis == dim else 1 for axis in range(len(shape))])
    return gain


def bell_draw(rng, dims, deviation, bound, cuts=(), kind=jnp.bfloat16):
    level = block_scale(rng, dims, cuts, -0.22, 0.18) if cuts else 1.0
    array = jax.random.normal(rng, dims, jnp.float32) * deviation * level
    return jnp.minimum(jnp.maximum(array, -bound), bound).astype(kind)


def setup_inputs(seed: int = 0) -> dict:
    arg_keys = jax.random.split(jax.random.key(seed), 8)
    a_blocks = bell_draw(arg_keys[0], (ROWS, SLOTS, BLOCK, BLOCK), (BLOCK * 4) ** -0.5, 0.25, ((0, 8), (1, 4)), jnp.float32)
    a_cols = draw_a_cols(jax.random.fold_in(arg_keys[7], 71), 0)
    a_lengths = draw_a_lengths(jax.random.fold_in(arg_keys[7], 71), 0)
    b_blocks = bell_draw(arg_keys[3], (NACT, N_ROW, BLOCK, BLOCK), 1.0, 6.0, ((0, 8), (1, 4)), jnp.float32)
    b_cols = touch_ends(jax.random.randint(arg_keys[4], (NACT, N_ROW), 0, WIN), jax.random.fold_in(arg_keys[4], 1), 0, WIN - 1).astype(jnp.int32)
    c_cols = draw_c_cols(jax.random.fold_in(arg_keys[7], 71), 0)
    order = jax.random.permutation(arg_keys[6], NACT).astype(jnp.int32)
    return {"a_blocks": a_blocks, "a_cols": a_cols, "a_lengths": a_lengths, "b_blocks": b_blocks, "b_cols": b_cols, "c_cols": c_cols, "order": order}


def reference(a_blocks, a_cols, a_lengths, b_blocks, b_cols, c_cols, order):
    position = order[a_cols]
    live_slots = jnp.arange(SLOTS, dtype=jnp.int32)[None, :] < a_lengths[:, None]
    group_count = c_cols.shape[1] // CSLOTS

    def one_row(packed):
        a_row, pos_row, live_row, pattern = packed
        chosen = b_blocks[pos_row].astype(jnp.float32)
        chosen_cols = b_cols[pos_row]
        pattern_two = pattern.reshape(group_count, CSLOTS)
        matches = (chosen_cols[:, :, None] == pattern_two[None, :, :]) & live_row[:, None, None]
        matches = matches.astype(jnp.float32)
        products = jnp.einsum("jab,jgbc->jgac", a_row.astype(jnp.float32), chosen,
                              precision=lax.Precision.HIGHEST)
        summed = jnp.einsum("jgs,jgac->gsac", matches, products, precision=lax.Precision.HIGHEST)
        return summed.reshape(group_count * CSLOTS, BLOCK, BLOCK)

    return lax.map(one_row, (a_blocks, position, live_slots, c_cols))
```

```python
import functools

import jax
import jax.numpy as jnp
from jax import lax
from jax.experimental import pallas as pl
from jax.experimental.pallas import tpu as pltpu
from jax.sharding import PartitionSpec as P

MESH = pl.DeviceIdType.MESH


def kernel(
    n_chip, n_col, chunk, a_cols, a_lengths, b_cols, c_cols, order, a_ref, b_ref, out_ref,
    a_all, b_all, b_split, acc,
    own_sem, out_sem, near_send, near_recv, far_send, far_recv, pass_send, pass_recv, b_send, b_recv,
):
    rows, slots, block = a_ref.shape[0], a_ref.shape[1], a_ref.shape[2]
    pattern = c_cols.shape[1]
    panels_each = b_ref.shape[0]
    panels = b_all.shape[0]
    chunks = rows // chunk
    me, my_col = lax.axis_index("row"), lax.axis_index("col")
    chip, core = me // 2, me % 2
    sibling = chip * 2 + 1 - core
    far = [lax.rem(chip + step, n_chip) * 2 + core for step in range(1, n_chip)]
    far_from = [lax.rem(chip + n_chip - step, n_chip) for step in range(1, n_chip)]
    peers_col = [lax.rem(my_col + step, n_col) for step in range(1, n_col)]
    from_col = [lax.rem(my_col + n_col - step, n_col) for step in range(1, n_col)]

    barrier = pltpu.get_barrier_semaphore()
    for peer in [sibling] + far:
        pl.semaphore_signal(barrier, inc=1, device_id={"row": peer}, device_id_type=MESH)
    for peer in peers_col:
        pl.semaphore_signal(barrier, inc=1, device_id={"col": peer}, device_id_type=MESH)
    pl.semaphore_wait(barrier, n_chip + n_col - 1)

    def part(t):
        return pl.ds(t * chunk, chunk)

    def own_copy():
        return pltpu.make_async_copy(a_ref, a_all.at[me], own_sem.at[0])

    def own_b():
        return pltpu.make_async_copy(b_ref, b_all.at[pl.ds(my_col * panels_each, panels_each)], own_sem.at[1])

    def near_copy(t):
        return pltpu.make_async_remote_copy(
            src_ref=a_ref.at[part(t)], dst_ref=a_all.at[me, part(t)],
            send_sem=near_send.at[t], recv_sem=near_recv.at[t],
            device_id={"row": sibling}, device_id_type=MESH,
        )

    def far_copy(k, t):
        return pltpu.make_async_remote_copy(
            src_ref=a_ref.at[part(t)], dst_ref=a_all.at[me, part(t)],
            send_sem=far_send.at[k, t], recv_sem=far_recv.at[k, t],
            device_id={"row": far[k]}, device_id_type=MESH,
        )

    def pass_copy(k, t):
        source = far_from[k] * 2 + core
        return pltpu.make_async_remote_copy(
            src_ref=a_all.at[source, part(t)], dst_ref=a_all.at[source, part(t)],
            send_sem=pass_send.at[k, t], recv_sem=pass_recv.at[k, t],
            device_id={"row": sibling}, device_id_type=MESH,
        )

    def b_copy(k):
        here = pl.ds(my_col * panels_each, panels_each)
        return pltpu.make_async_remote_copy(
            src_ref=b_ref, dst_ref=b_all.at[here],
            send_sem=b_send.at[k], recv_sem=b_recv.at[k],
            device_id={"col": peers_col[k]}, device_id_type=MESH,
        )

    def out_copy(t):
        return pltpu.make_async_copy(acc.at[part(t)], out_ref.at[part(t)], out_sem.at[t])

    for k in range(n_chip - 1):
        far_copy(k, 0).start()
    for k in range(n_col - 1):
        b_copy(k).start()
    own_b().start()

    @pl.loop(1, chunks)
    def _(t):
        for k in range(n_chip - 1):
            far_copy(k, t).start()

    own_copy().start()

    @pl.loop(0, chunks)
    def _(t):
        near_copy(t).start()

    own_b().wait()
    for k in range(n_col - 1):
        b_copy(k).wait_recv()

    @pl.loop(0, panels)
    def _(p):
        whole = b_all[p]
        high = whole.astype(jnp.bfloat16)
        low = (whole - high.astype(jnp.float32)).astype(jnp.bfloat16)
        both = jnp.concatenate([high, low], axis=1)
        b_split[p, :block, :] = both
        b_split[p, block:, :] = both

    def add_slots(i, source, first):
        products, marks = [], []
        for j in range(slots):
            slot = source * slots + j
            whole = a_all[source, i, j]
            high = whole.astype(jnp.bfloat16)
            low = (whole - high.astype(jnp.float32)).astype(jnp.bfloat16)
            position = order[a_cols[i, slot]]
            window = b_cols[position]
            live = slot < a_lengths[i]
            marks.append([
                jnp.where(jnp.logical_and(live, window == c_cols[i, s]), 1.0, 0.0).astype(jnp.float32)
                for s in range(pattern)
            ])
            wide = jnp.dot(
                jnp.concatenate([high, low], axis=1), b_split[position],
                preferred_element_type=jnp.float32,
            )
            products.append(wide[:, :block] + wide[:, block:])
        for s in range(pattern):
            total = marks[0][s] * products[0]
            for j in range(1, slots):
                total += marks[j][s] * products[j]
            if first:
                acc[i, s] = total
            else:
                acc[i, s] += total

    own_copy().wait()

    @pl.loop(0, chunks)
    def _(t):
        near_copy(t).wait_recv()

        @pl.loop(t * chunk, (t + 1) * chunk)
        def _(i):
            add_slots(i, me, True)
            add_slots(i, sibling, False)

    @pl.loop(0, chunks)
    def _(t):
        for k in range(n_chip - 1):
            far_copy(k, t).wait_recv()
            pass_copy(k, t).start()

        @pl.loop(t * chunk, (t + 1) * chunk)
        def _(i):
            for k in range(n_chip - 1):
                add_slots(i, far_from[k] * 2 + core, False)

        for k in range(n_chip - 1):
            pass_copy(k, t).wait_recv()

        @pl.loop(t * chunk, (t + 1) * chunk)
        def _(i):
            for k in range(n_chip - 1):
                add_slots(i, far_from[k] * 2 + 1 - core, False)

        out_copy(t).start()

    for k in range(n_col - 1):
        b_copy(k).wait_send()

    @pl.loop(0, chunks)
    def _(t):
        near_copy(t).wait_send()
        out_copy(t).wait()
        for k in range(n_chip - 1):
            far_copy(k, t).wait_send()
            pass_copy(k, t).wait_send()


def local(n_chip, n_col, a_blocks, a_cols, a_lengths, b_blocks, b_cols, c_cols, order):
    rows, slots, block = a_blocks.shape[0], a_blocks.shape[1], a_blocks.shape[2]
    pattern = c_cols.shape[1]
    panels_each = b_blocks.shape[0]
    panels = panels_each * n_col
    chunk = max(d for d in range(1, max(1, 4 // slots) + 1) if rows % d == 0)
    chunks = rows // chunk
    smem = pl.BlockSpec(memory_space=pltpu.SMEM)
    hbm = pl.BlockSpec(memory_space=pl.ANY)
    dma = pltpu.SemaphoreType.DMA
    return pl.pallas_call(
        functools.partial(kernel, n_chip, n_col, chunk),
        out_shape=jax.ShapeDtypeStruct((rows, pattern, block, block), jnp.float32),
        in_specs=[smem] * 5 + [hbm] * 2,
        out_specs=hbm,
        scratch_shapes=[
            pltpu.VMEM((n_chip * 2, rows, slots, block, block), jnp.float32),
            pltpu.VMEM((panels, block, block), jnp.float32),
            pltpu.VMEM((panels, 2 * block, 2 * block), jnp.bfloat16),
            pltpu.VMEM((rows, pattern, block, block), jnp.float32),
            dma((2,)),
            dma((chunks,)),
            dma((chunks,)),
            dma((chunks,)),
            dma((n_chip - 1, chunks)),
            dma((n_chip - 1, chunks)),
            dma((n_chip - 1, chunks)),
            dma((n_chip - 1, chunks)),
            dma((n_col - 1,)),
            dma((n_col - 1,)),
        ],
        compiler_params=pltpu.CompilerParams(
            collective_id=0, has_side_effects=True, vmem_limit_bytes=56 * 1024 * 1024
        ),
        cost_estimate=pl.CostEstimate(
            flops=2 * rows * slots * 2 * n_chip * 4 * block**3,
            bytes_accessed=4 * rows * block * block * (slots + pattern),
            transcendentals=0,
        ),
    )(a_cols, a_lengths, b_cols.reshape(-1), c_cols, order, a_blocks, b_blocks.reshape(panels_each, block, block))


def solution(mesh):
    return jax.shard_map(
        functools.partial(local, mesh.shape["row"] // 2, mesh.shape["col"]),
        mesh=mesh,
        in_specs=(
            P("col", "row", None, None),
            P("col", None),
            P("col"),
            P("col", "row", None, None),
            P(None, "row"),
            P("col", "row"),
            P(),
        ),
        out_specs=P("col", "row", None, None),
        check_vma=False,
    )
```

```python
import functools

import jax
import jax.numpy as jnp
from jax import lax
from jax.experimental import pallas as pl
from jax.experimental.pallas import tpu as pltpu
from jax.sharding import PartitionSpec as P

MESH = pl.DeviceIdType.MESH


def kernel(
    n_chip, n_col, chunk, a_cols, a_lengths, b_cols, c_cols, order, a_ref, b_ref, acc,
    a_all, b_all, b_split,
    own_sem, near_send, near_recv, far_send, far_recv, pass_send, pass_recv, b_send, b_recv,
):
    rows, slots, block = a_ref.shape[0], a_ref.shape[1], a_ref.shape[2]
    pattern = c_cols.shape[0]
    panels_each = b_ref.shape[0]
    panels = b_all.shape[0]
    chunks = rows // chunk
    me, my_col = lax.axis_index("row"), lax.axis_index("col")
    chip, core = me // 2, me % 2
    sibling = chip * 2 + 1 - core
    far = [lax.rem(chip + step, n_chip) * 2 + core for step in range(1, n_chip)]
    far_from = [lax.rem(chip + n_chip - step, n_chip) for step in range(1, n_chip)]
    peers_col = [lax.rem(my_col + step, n_col) for step in range(1, n_col)]
    from_col = [lax.rem(my_col + n_col - step, n_col) for step in range(1, n_col)]

    barrier = pltpu.get_barrier_semaphore()
    for peer in [sibling] + far:
        pl.semaphore_signal(barrier, inc=1, device_id={"row": peer}, device_id_type=MESH)
    for peer in peers_col:
        pl.semaphore_signal(barrier, inc=1, device_id={"col": peer}, device_id_type=MESH)
    pl.semaphore_wait(barrier, n_chip + n_col - 1)

    def part(t):
        return pl.ds(t * chunk, chunk)

    def own_copy():
        return pltpu.make_async_copy(a_ref, a_all.at[me], own_sem.at[0])

    def own_b():
        return pltpu.make_async_copy(b_ref, b_all.at[pl.ds(my_col * panels_each, panels_each)], own_sem.at[1])

    def near_copy(t):
        return pltpu.make_async_remote_copy(
            src_ref=a_ref.at[part(t)], dst_ref=a_all.at[me, part(t)],
            send_sem=near_send.at[t], recv_sem=near_recv.at[t],
            device_id={"row": sibling}, device_id_type=MESH,
        )

    def far_copy(k, t):
        return pltpu.make_async_remote_copy(
            src_ref=a_ref.at[part(t)], dst_ref=a_all.at[me, part(t)],
            send_sem=far_send.at[k, t], recv_sem=far_recv.at[k, t],
            device_id={"row": far[k]}, device_id_type=MESH,
        )

    def pass_copy(k, t):
        source = far_from[k] * 2 + core
        return pltpu.make_async_remote_copy(
            src_ref=a_all.at[source, part(t)], dst_ref=a_all.at[source, part(t)],
            send_sem=pass_send.at[k, t], recv_sem=pass_recv.at[k, t],
            device_id={"row": sibling}, device_id_type=MESH,
        )

    def b_copy(k):
        here = pl.ds(my_col * panels_each, panels_each)
        return pltpu.make_async_remote_copy(
            src_ref=b_ref, dst_ref=b_all.at[here],
            send_sem=b_send.at[k], recv_sem=b_recv.at[k],
            device_id={"col": peers_col[k]}, device_id_type=MESH,
        )

    own_b().start()
    own_copy().start()
    sent_b = 0
    for t in range(chunks):
        for k in range(n_chip - 1):
            far_copy(k, t).start()
        upto = (n_col - 1) * (t + 1) // min(chunks, n_col - 1) if t + 1 < chunks else n_col - 1
        for k in range(sent_b, min(upto, n_col - 1)):
            b_copy(k).start()
        sent_b = min(upto, n_col - 1)

    @pl.loop(0, chunks)
    def _(t):
        near_copy(t).start()

    own_b().wait()
    for k in range(n_col - 1):
        b_copy(k).wait_recv()

    @pl.loop(0, panels)
    def _(p):
        whole = b_all[p]
        high = whole.astype(jnp.bfloat16)
        low = (whole - high.astype(jnp.float32)).astype(jnp.bfloat16)
        both = jnp.concatenate([high, low], axis=1)
        b_split[p, :block, :] = both
        b_split[p, block:, :] = both

    def add_slots(i, source, first):
        products, marks = [], []
        for j in range(slots):
            slot = source * slots + j
            whole = a_all[source, i, j]
            high = whole.astype(jnp.bfloat16)
            low = (whole - high.astype(jnp.float32)).astype(jnp.bfloat16)
            position = order[a_cols[i, slot]]
            window = b_cols[position]
            live = slot < a_lengths[i]
            marks.append([
                jnp.where(jnp.logical_and(live, window == c_cols[s, i]), 1.0, 0.0).astype(jnp.float32)
                for s in range(pattern)
            ])
            wide = jnp.dot(
                jnp.concatenate([high, low], axis=1), b_split[position],
                preferred_element_type=jnp.float32,
            )
            products.append(wide[:, :block] + wide[:, block:])
        for s in range(pattern):
            total = marks[0][s] * products[0]
            for j in range(1, slots):
                total += marks[j][s] * products[j]
            if first:
                acc[i, s] = total
            else:
                acc[i, s] += total

    own_copy().wait()

    @pl.loop(0, chunks)
    def _(t):
        near_copy(t).wait_recv()

        @pl.loop(t * chunk, (t + 1) * chunk)
        def _(i):
            add_slots(i, me, True)
            add_slots(i, sibling, False)

    @pl.loop(0, chunks)
    def _(t):
        for k in range(n_chip - 1):
            far_copy(k, t).wait_recv()
            pass_copy(k, t).start()

        @pl.loop(t * chunk, (t + 1) * chunk)
        def _(i):
            for k in range(n_chip - 1):
                add_slots(i, far_from[k] * 2 + core, False)

        for k in range(n_chip - 1):
            pass_copy(k, t).wait_recv()

        @pl.loop(t * chunk, (t + 1) * chunk)
        def _(i):
            for k in range(n_chip - 1):
                add_slots(i, far_from[k] * 2 + 1 - core, False)

    for k in range(n_col - 1):
        b_copy(k).wait_send()

    @pl.loop(0, chunks)
    def _(t):
        near_copy(t).wait_send()
        for k in range(n_chip - 1):
            far_copy(k, t).wait_send()
            pass_copy(k, t).wait_send()


def local(n_chip, n_col, a_blocks, a_cols, a_lengths, b_blocks, b_cols, c_cols, order):
    rows, slots, block = a_blocks.shape[0], a_blocks.shape[1], a_blocks.shape[2]
    pattern = c_cols.shape[1]
    panels_each = b_blocks.shape[0]
    panels = panels_each * n_col
    chunk = max(d for d in range(1, max(1, 4 // slots) + 1) if rows % d == 0)
    chunks = rows // chunk
    smem = pl.BlockSpec(memory_space=pltpu.SMEM)
    hbm = pl.BlockSpec(memory_space=pl.ANY)
    dma = pltpu.SemaphoreType.DMA
    return pl.pallas_call(
        functools.partial(kernel, n_chip, n_col, chunk),
        out_shape=pltpu.VMEM((rows, pattern, block, block), jnp.float32),
        in_specs=[smem] * 5 + [hbm] * 2,
        out_specs=pl.BlockSpec(memory_space=pltpu.VMEM),
        scratch_shapes=[
            pltpu.VMEM((n_chip * 2, rows, slots, block, block), jnp.float32),
            pltpu.VMEM((panels, block, block), jnp.float32),
            pltpu.VMEM((panels, 2 * block, 2 * block), jnp.bfloat16),
            dma((2,)),
            dma((chunks,)),
            dma((chunks,)),
            dma((n_chip - 1, chunks)),
            dma((n_chip - 1, chunks)),
            dma((n_chip - 1, chunks)),
            dma((n_chip - 1, chunks)),
            dma((n_col - 1,)),
            dma((n_col - 1,)),
        ],
        compiler_params=pltpu.CompilerParams(
            collective_id=0, has_side_effects=True, vmem_limit_bytes=60 * 1024 * 1024
        ),
        cost_estimate=pl.CostEstimate(
            flops=2 * rows * slots * 2 * n_chip * 4 * block**3,
            bytes_accessed=4 * rows * block * block * (slots + pattern),
            transcendentals=0,
        ),
    )(a_cols, a_lengths, b_cols.reshape(-1), c_cols.T, order, a_blocks, b_blocks.reshape(panels_each, block, block))


def solution(mesh):
    return jax.shard_map(
        functools.partial(local, mesh.shape["row"] // 2, mesh.shape["col"]),
        mesh=mesh,
        in_specs=(
            P("col", "row", None, None),
            P("col", None),
            P("col"),
            P("col", "row", None, None),
            P(None, "row"),
            P("col", "row"),
            P(),
        ),
        out_specs=P("col", "row", None, None),
        check_vma=False,
    )
```

```python
import functools

import jax
import jax.numpy as jnp
from jax import lax
from jax.experimental import pallas as pl
from jax.experimental.pallas import tpu as pltpu
from jax.sharding import PartitionSpec as P

MESH = pl.DeviceIdType.MESH


def ring_spot(col, n_col):
    odd = col % 2
    return (1 - odd) * (col // 2) + odd * (n_col - 1 - col // 2)


def ring_col(spot, n_col):
    back = spot // (n_col // 2)
    return (1 - back) * (2 * spot) + back * (2 * (n_col - 1 - spot) + 1)


def kernel(
    n_chip, n_col, chunk, a_cols, a_lengths, b_cols, c_cols, order, a_ref, b_ref, acc,
    a_all, b_all, b_split,
    own_sem, near_send, near_recv, far_send, far_recv, pass_send, pass_recv, b_send, b_recv,
):
    rows, slots, block = a_ref.shape[0], a_ref.shape[1], a_ref.shape[2]
    pattern = c_cols.shape[0]
    panels_each = b_ref.shape[0]
    panels = b_all.shape[0]
    chunks = rows // chunk
    me, my_col = lax.axis_index("row"), lax.axis_index("col")
    chip, core = me // 2, me % 2
    sibling = chip * 2 + 1 - core
    far = [lax.rem(chip + step, n_chip) * 2 + core for step in range(1, n_chip)]
    far_from = [lax.rem(chip + n_chip - step, n_chip) for step in range(1, n_chip)]
    spot = ring_spot(my_col, n_col)
    ring = [ring_col(lax.rem(spot + step, n_col), n_col) for step in (1, n_col - 1)]
    hops = (n_col // 2, (n_col - 1) // 2)

    barrier = pltpu.get_barrier_semaphore()
    for peer in [sibling] + far:
        pl.semaphore_signal(barrier, inc=1, device_id={"row": peer}, device_id_type=MESH)
    for peer in ring:
        pl.semaphore_signal(barrier, inc=1, device_id={"col": peer}, device_id_type=MESH)
    pl.semaphore_wait(barrier, n_chip + 2)

    def part(t):
        return pl.ds(t * chunk, chunk)

    def own_copy():
        return pltpu.make_async_copy(a_ref, a_all.at[me], own_sem.at[0])

    def own_b():
        return pltpu.make_async_copy(b_ref, b_all.at[pl.ds(my_col * panels_each, panels_each)], own_sem.at[1])

    def near_copy(t):
        return pltpu.make_async_remote_copy(
            src_ref=a_ref.at[part(t)], dst_ref=a_all.at[me, part(t)],
            send_sem=near_send.at[t], recv_sem=near_recv.at[t],
            device_id={"row": sibling}, device_id_type=MESH,
        )

    def far_copy(k, t):
        return pltpu.make_async_remote_copy(
            src_ref=a_ref.at[part(t)], dst_ref=a_all.at[me, part(t)],
            send_sem=far_send.at[k, t], recv_sem=far_recv.at[k, t],
            device_id={"row": far[k]}, device_id_type=MESH,
        )

    def pass_copy(k, t):
        source = far_from[k] * 2 + core
        return pltpu.make_async_remote_copy(
            src_ref=a_all.at[source, part(t)], dst_ref=a_all.at[source, part(t)],
            send_sem=pass_send.at[k, t], recv_sem=pass_recv.at[k, t],
            device_id={"row": sibling}, device_id_type=MESH,
        )

    def b_copy(way, hop):
        back = hop if way == 1 else n_col - hop
        here = pl.ds(ring_col(lax.rem(spot + back, n_col), n_col) * panels_each, panels_each)
        return pltpu.make_async_remote_copy(
            src_ref=b_all.at[here], dst_ref=b_all.at[here],
            send_sem=b_send.at[way, hop], recv_sem=b_recv.at[way, hop],
            device_id={"col": ring[way]}, device_id_type=MESH,
        )

    own_b().start()

    @pl.loop(0, chunks)
    def _(t):
        for k in range(n_chip - 1):
            far_copy(k, t).start()

    own_b().wait()
    for way in (0, 1):
        b_copy(way, 0).start()
    own_copy().start()

    @pl.loop(0, chunks)
    def _(t):
        near_copy(t).start()

    for way in (0, 1):
        b_copy(way, 0).wait_recv()
    for hop in range(1, hops[0]):
        for way in (0, 1):
            if hop < hops[way]:
                b_copy(way, hop).start()
        for way in (0, 1):
            if hop < hops[way]:
                b_copy(way, hop).wait_recv()

    @pl.loop(0, panels)
    def _(p):
        whole = b_all[p]
        high = whole.astype(jnp.bfloat16)
        low = (whole - high.astype(jnp.float32)).astype(jnp.bfloat16)
        both = jnp.concatenate([high, low], axis=1)
        b_split[p, :block, :] = both
        b_split[p, block:, :] = both

    def add_slots(i, source, first):
        products, marks = [], []
        for j in range(slots):
            slot = source * slots + j
            whole = a_all[source, i, j]
            high = whole.astype(jnp.bfloat16)
            low = (whole - high.astype(jnp.float32)).astype(jnp.bfloat16)
            position = order[a_cols[i, slot]]
            window = b_cols[position]
            live = slot < a_lengths[i]
            marks.append([
                jnp.where(jnp.logical_and(live, window == c_cols[s, i]), 1.0, 0.0).astype(jnp.float32)
                for s in range(pattern)
            ])
            wide = jnp.dot(
                jnp.concatenate([high, low], axis=1), b_split[position],
                preferred_element_type=jnp.float32,
            )
            products.append(wide[:, :block] + wide[:, block:])
        for s in range(pattern):
            total = marks[0][s] * products[0]
            for j in range(1, slots):
                total += marks[j][s] * products[j]
            if first:
                acc[i, s] = total
            else:
                acc[i, s] += total

    own_copy().wait()

    @pl.loop(0, chunks)
    def _(t):
        near_copy(t).wait_recv()

        @pl.loop(t * chunk, (t + 1) * chunk)
        def _(i):
            add_slots(i, me, True)
            add_slots(i, sibling, False)

    @pl.loop(0, chunks)
    def _(t):
        for k in range(n_chip - 1):
            far_copy(k, t).wait_recv()
            pass_copy(k, t).start()

        @pl.loop(t * chunk, (t + 1) * chunk)
        def _(i):
            for k in range(n_chip - 1):
                add_slots(i, far_from[k] * 2 + core, False)

        for k in range(n_chip - 1):
            pass_copy(k, t).wait_recv()

        @pl.loop(t * chunk, (t + 1) * chunk)
        def _(i):
            for k in range(n_chip - 1):
                add_slots(i, far_from[k] * 2 + 1 - core, False)

    for way in (0, 1):
        for hop in range(hops[way]):
            b_copy(way, hop).wait_send()

    @pl.loop(0, chunks)
    def _(t):
        near_copy(t).wait_send()
        for k in range(n_chip - 1):
            far_copy(k, t).wait_send()
            pass_copy(k, t).wait_send()


def local(n_chip, n_col, a_blocks, a_cols, a_lengths, b_blocks, b_cols, c_cols, order):
    rows, slots, block = a_blocks.shape[0], a_blocks.shape[1], a_blocks.shape[2]
    pattern = c_cols.shape[1]
    panels_each = b_blocks.shape[0]
    panels = panels_each * n_col
    chunk = max(d for d in range(1, max(1, 4 // slots) + 1) if rows % d == 0)
    chunks = rows // chunk
    smem = pl.BlockSpec(memory_space=pltpu.SMEM)
    hbm = pl.BlockSpec(memory_space=pl.ANY)
    dma = pltpu.SemaphoreType.DMA
    return pl.pallas_call(
        functools.partial(kernel, n_chip, n_col, chunk),
        out_shape=pltpu.VMEM((rows, pattern, block, block), jnp.float32),
        in_specs=[smem] * 5 + [hbm] * 2,
        out_specs=pl.BlockSpec(memory_space=pltpu.VMEM),
        scratch_shapes=[
            pltpu.VMEM((n_chip * 2, rows, slots, block, block), jnp.float32),
            pltpu.VMEM((panels, block, block), jnp.float32),
            pltpu.VMEM((panels, 2 * block, 2 * block), jnp.bfloat16),
            dma((2,)),
            dma((chunks,)),
            dma((chunks,)),
            dma((n_chip - 1, chunks)),
            dma((n_chip - 1, chunks)),
            dma((n_chip - 1, chunks)),
            dma((n_chip - 1, chunks)),
            dma((2, n_col // 2)),
            dma((2, n_col // 2)),
        ],
        compiler_params=pltpu.CompilerParams(
            collective_id=0, has_side_effects=True, vmem_limit_bytes=60 * 1024 * 1024
        ),
        cost_estimate=pl.CostEstimate(
            flops=2 * rows * slots * 2 * n_chip * 4 * block**3,
            bytes_accessed=4 * rows * block * block * (slots + pattern),
            transcendentals=0,
        ),
    )(a_cols, a_lengths, b_cols.reshape(-1), c_cols.T, order, a_blocks, b_blocks.reshape(panels_each, block, block))


def solution(mesh):
    return jax.shard_map(
        functools.partial(local, mesh.shape["row"] // 2, mesh.shape["col"]),
        mesh=mesh,
        in_specs=(
            P("col", "row", None, None),
            P("col", None),
            P("col"),
            P("col", "row", None, None),
            P(None, "row"),
            P("col", "row"),
            P(),
        ),
        out_specs=P("col", "row", None, None),
        check_vma=False,
    )
```

```python
import functools

import jax
import jax.numpy as jnp
from jax import lax
from jax.experimental import pallas as pl
from jax.experimental.pallas import tpu as pltpu
from jax.sharding import PartitionSpec as P

MESH = pl.DeviceIdType.MESH


def ring_spot(col, n_col):
    odd = col % 2
    return (1 - odd) * (col // 2) + odd * (n_col - 1 - col // 2)


def ring_col(spot, n_col):
    back = spot // (n_col // 2)
    return (1 - back) * (2 * spot) + back * (2 * (n_col - 1 - spot) + 1)


def cut(rows, slots):
    pieces, row = [], 0
    while row < rows - 1:
        size = (rows - 1 - row + 2) // 3
        pieces.append((row, size, 0, slots))
        row += size
    slot = 0
    while slot < slots:
        size = (slots - slot + 1) // 2
        pieces.append((row, 1, slot, size))
        slot += size
    return pieces


def kernel(
    n_chip, n_col, chunk, a_cols, a_lengths, b_cols, c_cols, order, a_ref, b_ref, acc,
    a_all, b_all, b_split,
    own_sem, near_send, near_recv, far_send, far_recv, pass_send, pass_recv, b_send, b_recv,
):
    rows, slots, block = a_ref.shape[0], a_ref.shape[1], a_ref.shape[2]
    pattern = c_cols.shape[0]
    panels_each = b_ref.shape[0]
    panels = b_all.shape[0]
    chunks = rows // chunk
    me, my_col = lax.axis_index("row"), lax.axis_index("col")
    chip, core = me // 2, me % 2
    sibling = chip * 2 + 1 - core
    far = [lax.rem(chip + step, n_chip) * 2 + core for step in range(1, n_chip)]
    far_from = [lax.rem(chip + n_chip - step, n_chip) for step in range(1, n_chip)]
    spot = ring_spot(my_col, n_col)
    ring = [ring_col(lax.rem(spot + step, n_col), n_col) for step in (1, n_col - 1)]
    hops = (n_col // 2, (n_col - 1) // 2)

    barrier = pltpu.get_barrier_semaphore()
    for peer in [sibling] + far:
        pl.semaphore_signal(barrier, inc=1, device_id={"row": peer}, device_id_type=MESH)
    for peer in ring:
        pl.semaphore_signal(barrier, inc=1, device_id={"col": peer}, device_id_type=MESH)
    pl.semaphore_wait(barrier, n_chip + 2)

    def part(t):
        return pl.ds(t * chunk, chunk)

    def own_copy():
        return pltpu.make_async_copy(a_ref, a_all.at[me], own_sem.at[0])

    def own_b():
        return pltpu.make_async_copy(b_ref, b_all.at[pl.ds(my_col * panels_each, panels_each)], own_sem.at[1])

    def near_copy(t):
        return pltpu.make_async_remote_copy(
            src_ref=a_ref.at[part(t)], dst_ref=a_all.at[me, part(t)],
            send_sem=near_send.at[t], recv_sem=near_recv.at[t],
            device_id={"row": sibling}, device_id_type=MESH,
        )

    pieces = cut(rows, slots)

    def piece(p):
        row, row_count, slot, slot_count = pieces[p]
        return pl.ds(row, row_count), pl.ds(slot, slot_count)

    def far_copy(k, t):
        return pltpu.make_async_remote_copy(
            src_ref=a_ref.at[piece(t)], dst_ref=a_all.at[(me,) + piece(t)],
            send_sem=far_send.at[k, t], recv_sem=far_recv.at[k, t],
            device_id={"row": far[k]}, device_id_type=MESH,
        )

    def pass_copy(k, t):
        source = far_from[k] * 2 + core
        return pltpu.make_async_remote_copy(
            src_ref=a_all.at[(source,) + piece(t)], dst_ref=a_all.at[(source,) + piece(t)],
            send_sem=pass_send.at[k, t], recv_sem=pass_recv.at[k, t],
            device_id={"row": sibling}, device_id_type=MESH,
        )

    def b_copy(way, hop):
        back = hop if way == 1 else n_col - hop
        here = pl.ds(ring_col(lax.rem(spot + back, n_col), n_col) * panels_each, panels_each)
        return pltpu.make_async_remote_copy(
            src_ref=b_all.at[here], dst_ref=b_all.at[here],
            send_sem=b_send.at[way, hop], recv_sem=b_recv.at[way, hop],
            device_id={"col": ring[way]}, device_id_type=MESH,
        )

    own_b().start()

    for t in range(len(pieces)):
        for k in range(n_chip - 1):
            far_copy(k, t).start()

    own_b().wait()
    for way in (0, 1):
        b_copy(way, 0).start()
    own_copy().start()

    @pl.loop(0, chunks)
    def _(t):
        near_copy(t).start()

    for way in (0, 1):
        b_copy(way, 0).wait_recv()
    for hop in range(1, hops[0]):
        for way in (0, 1):
            if hop < hops[way]:
                b_copy(way, hop).start()
        for way in (0, 1):
            if hop < hops[way]:
                b_copy(way, hop).wait_recv()

    @pl.loop(0, panels)
    def _(p):
        whole = b_all[p]
        high = whole.astype(jnp.bfloat16)
        low = (whole - high.astype(jnp.float32)).astype(jnp.bfloat16)
        both = jnp.concatenate([high, low], axis=1)
        b_split[p, :block, :] = both
        b_split[p, block:, :] = both

    def add_slots(i, source, first, start=0, count=slots):
        products, marks = [], []
        for j in range(start, start + count):
            slot = source * slots + j
            whole = a_all[source, i, j]
            high = whole.astype(jnp.bfloat16)
            low = (whole - high.astype(jnp.float32)).astype(jnp.bfloat16)
            position = order[a_cols[i, slot]]
            window = b_cols[position]
            live = slot < a_lengths[i]
            marks.append([
                jnp.where(jnp.logical_and(live, window == c_cols[s, i]), 1.0, 0.0).astype(jnp.float32)
                for s in range(pattern)
            ])
            wide = jnp.dot(
                jnp.concatenate([high, low], axis=1), b_split[position],
                preferred_element_type=jnp.float32,
            )
            products.append(wide[:, :block] + wide[:, block:])
        for s in range(pattern):
            total = marks[0][s] * products[0]
            for j in range(1, count):
                total += marks[j][s] * products[j]
            if first:
                acc[i, s] = total
            else:
                acc[i, s] += total

    own_copy().wait()

    @pl.loop(0, chunks)
    def _(t):
        near_copy(t).wait_recv()

        @pl.loop(t * chunk, (t + 1) * chunk)
        def _(i):
            add_slots(i, me, True)
            add_slots(i, sibling, False)

    def add_piece(p, side):
        row, row_count, slot, slot_count = pieces[p]

        @pl.loop(row, row + row_count)
        def _(i):
            for k in range(n_chip - 1):
                add_slots(i, far_from[k] * 2 + side, False, slot, slot_count)

    for t in range(len(pieces)):
        for k in range(n_chip - 1):
            far_copy(k, t).wait_recv()
            pass_copy(k, t).start()
        if t > 0:
            for k in range(n_chip - 1):
                pass_copy(k, t - 1).wait_recv()
            add_piece(t - 1, 1 - core)
        add_piece(t, core)
    for k in range(n_chip - 1):
        pass_copy(k, len(pieces) - 1).wait_recv()
    add_piece(len(pieces) - 1, 1 - core)

    for way in (0, 1):
        for hop in range(hops[way]):
            b_copy(way, hop).wait_send()

    @pl.loop(0, chunks)
    def _(t):
        near_copy(t).wait_send()

    for t in range(len(pieces)):
        for k in range(n_chip - 1):
            far_copy(k, t).wait_send()
            pass_copy(k, t).wait_send()


def local(n_chip, n_col, a_blocks, a_cols, a_lengths, b_blocks, b_cols, c_cols, order):
    rows, slots, block = a_blocks.shape[0], a_blocks.shape[1], a_blocks.shape[2]
    pattern = c_cols.shape[1]
    panels_each = b_blocks.shape[0]
    panels = panels_each * n_col
    chunk = max(d for d in range(1, max(1, 4 // slots) + 1) if rows % d == 0)
    chunks = rows // chunk
    smem = pl.BlockSpec(memory_space=pltpu.SMEM)
    hbm = pl.BlockSpec(memory_space=pl.ANY)
    dma = pltpu.SemaphoreType.DMA
    return pl.pallas_call(
        functools.partial(kernel, n_chip, n_col, chunk),
        out_shape=pltpu.VMEM((rows, pattern, block, block), jnp.float32),
        in_specs=[smem] * 5 + [hbm] * 2,
        out_specs=pl.BlockSpec(memory_space=pltpu.VMEM),
        scratch_shapes=[
            pltpu.VMEM((n_chip * 2, rows, slots, block, block), jnp.float32),
            pltpu.VMEM((panels, block, block), jnp.float32),
            pltpu.VMEM((panels, 2 * block, 2 * block), jnp.bfloat16),
            dma((2,)),
            dma((chunks,)),
            dma((chunks,)),
            dma((n_chip - 1, len(cut(rows, slots)))),
            dma((n_chip - 1, len(cut(rows, slots)))),
            dma((n_chip - 1, len(cut(rows, slots)))),
            dma((n_chip - 1, len(cut(rows, slots)))),
            dma((2, n_col // 2)),
            dma((2, n_col // 2)),
        ],
        compiler_params=pltpu.CompilerParams(
            collective_id=0, has_side_effects=True, vmem_limit_bytes=60 * 1024 * 1024
        ),
        cost_estimate=pl.CostEstimate(
            flops=2 * rows * slots * 2 * n_chip * 4 * block**3,
            bytes_accessed=4 * rows * block * block * (slots + pattern),
            transcendentals=0,
        ),
    )(a_cols, a_lengths, b_cols.reshape(-1), c_cols.T, order, a_blocks, b_blocks.reshape(panels_each, block, block))


def solution(mesh):
    return jax.shard_map(
        functools.partial(local, mesh.shape["row"] // 2, mesh.shape["col"]),
        mesh=mesh,
        in_specs=(
            P("col", "row", None, None),
            P("col", None),
            P("col"),
            P("col", "row", None, None),
            P(None, "row"),
            P("col", "row"),
            P(),
        ),
        out_specs=P("col", "row", None, None),
        check_vma=False,
    )
```

```python
import functools

import jax
import jax.numpy as jnp
from jax import lax
from jax.experimental import pallas as pl
from jax.experimental.pallas import tpu as pltpu
from jax.sharding import PartitionSpec as P

MESH = pl.DeviceIdType.MESH


def ring_spot(col, n_col):
    odd = col % 2
    return (1 - odd) * (col // 2) + odd * (n_col - 1 - col // 2)


def ring_col(spot, n_col):
    back = spot // (n_col // 2)
    return (1 - back) * (2 * spot) + back * (2 * (n_col - 1 - spot) + 1)


def cut(rows, slots):
    pieces, row = [], 0
    while row < rows - 1:
        size = (rows - 1 - row + 2) // 3
        pieces.append((row, size, 0, slots))
        row += size
    slot = 0
    while slot < slots:
        size = (slots - slot + 1) // 2
        pieces.append((row, 1, slot, size))
        slot += size
    return pieces


def kernel(
    n_chip, n_col, chunk, a_cols, a_lengths, b_cols, c_cols, order, a_ref, b_ref, acc,
    a_all, b_all, b_split,
    own_sem, near_send, near_recv, far_send, far_recv, pass_send, pass_recv, b_send, b_recv,
):
    rows, slots, block = a_ref.shape[0], a_ref.shape[1], a_ref.shape[2]
    pattern = c_cols.shape[0]
    panels_each = b_ref.shape[0]
    panels = b_all.shape[0]
    chunks = rows // chunk
    me, my_col = lax.axis_index("row"), lax.axis_index("col")
    chip, core = me // 2, me % 2
    sibling = chip * 2 + 1 - core
    far = [lax.rem(chip + step, n_chip) * 2 + core for step in range(1, n_chip)]
    far_from = [lax.rem(chip + n_chip - step, n_chip) for step in range(1, n_chip)]
    spot = ring_spot(my_col, n_col)
    ring = [ring_col(lax.rem(spot + step, n_col), n_col) for step in (1, n_col - 1)]
    hops = (n_col // 2, (n_col - 1) // 2)

    barrier = pltpu.get_barrier_semaphore()
    for peer in [sibling] + far:
        pl.semaphore_signal(barrier, inc=1, device_id={"row": peer}, device_id_type=MESH)
    for peer in ring:
        pl.semaphore_signal(barrier, inc=1, device_id={"col": peer}, device_id_type=MESH)
    pl.semaphore_wait(barrier, n_chip + 2)

    def part(t):
        return pl.ds(t * chunk, chunk)

    def own_copy():
        return pltpu.make_async_copy(a_ref, a_all.at[me], own_sem.at[0])

    def own_b():
        return pltpu.make_async_copy(b_ref, b_all.at[pl.ds(my_col * panels_each, panels_each)], own_sem.at[1])

    def near_copy(t):
        return pltpu.make_async_remote_copy(
            src_ref=a_all.at[me, part(t)], dst_ref=a_all.at[me, part(t)],
            send_sem=near_send.at[t], recv_sem=near_recv.at[t],
            device_id={"row": sibling}, device_id_type=MESH,
        )

    pieces = cut(rows, slots)

    def piece(p):
        row, row_count, slot, slot_count = pieces[p]
        return pl.ds(row, row_count), pl.ds(slot, slot_count)

    def far_copy(k, t):
        return pltpu.make_async_remote_copy(
            src_ref=a_ref.at[piece(t)] if t == 0 else a_all.at[(me,) + piece(t)], dst_ref=a_all.at[(me,) + piece(t)],
            send_sem=far_send.at[k, t], recv_sem=far_recv.at[k, t],
            device_id={"row": far[k]}, device_id_type=MESH,
        )

    def pass_copy(k, t):
        source = far_from[k] * 2 + core
        return pltpu.make_async_remote_copy(
            src_ref=a_all.at[(source,) + piece(t)], dst_ref=a_all.at[(source,) + piece(t)],
            send_sem=pass_send.at[k, t], recv_sem=pass_recv.at[k, t],
            device_id={"row": sibling}, device_id_type=MESH,
        )

    def b_copy(way, hop):
        back = hop if way == 1 else n_col - hop
        here = pl.ds(ring_col(lax.rem(spot + back, n_col), n_col) * panels_each, panels_each)
        return pltpu.make_async_remote_copy(
            src_ref=b_all.at[here], dst_ref=b_all.at[here],
            send_sem=b_send.at[way, hop], recv_sem=b_recv.at[way, hop],
            device_id={"col": ring[way]}, device_id_type=MESH,
        )

    own_b().start()

    own_copy().start()
    for k in range(n_chip - 1):
        far_copy(k, 0).start()
    own_b().wait()
    for way in (0, 1):
        b_copy(way, 0).start()
    own_copy().wait()
    for t in range(1, len(pieces)):
        for k in range(n_chip - 1):
            far_copy(k, t).start()

    @pl.loop(0, chunks)
    def _(t):
        near_copy(t).start()

    for way in (0, 1):
        b_copy(way, 0).wait_recv()
    for hop in range(1, hops[0]):
        for way in (0, 1):
            if hop < hops[way]:
                b_copy(way, hop).start()
        for way in (0, 1):
            if hop < hops[way]:
                b_copy(way, hop).wait_recv()

    @pl.loop(0, panels)
    def _(p):
        whole = b_all[p]
        high = whole.astype(jnp.bfloat16)
        low = (whole - high.astype(jnp.float32)).astype(jnp.bfloat16)
        both = jnp.concatenate([high, low], axis=1)
        b_split[p, :block, :] = both
        b_split[p, block:, :] = both

    def add_slots(i, source, first, start=0, count=slots):
        products, marks = [], []
        for j in range(start, start + count):
            slot = source * slots + j
            whole = a_all[source, i, j]
            high = whole.astype(jnp.bfloat16)
            low = (whole - high.astype(jnp.float32)).astype(jnp.bfloat16)
            position = order[a_cols[i, slot]]
            window = b_cols[position]
            live = slot < a_lengths[i]
            marks.append([
                jnp.where(jnp.logical_and(live, window == c_cols[s, i]), 1.0, 0.0).astype(jnp.float32)
                for s in range(pattern)
            ])
            wide = jnp.dot(
                jnp.concatenate([high, low], axis=1), b_split[position],
                preferred_element_type=jnp.float32,
            )
            products.append(wide[:, :block] + wide[:, block:])
        for s in range(pattern):
            total = marks[0][s] * products[0]
            for j in range(1, count):
                total += marks[j][s] * products[j]
            if first:
                acc[i, s] = total
            else:
                acc[i, s] += total

    @pl.loop(0, chunks)
    def _(t):
        near_copy(t).wait_recv()

        @pl.loop(t * chunk, (t + 1) * chunk)
        def _(i):
            add_slots(i, me, True)
            add_slots(i, sibling, False)

    def add_piece(p, side):
        row, row_count, slot, slot_count = pieces[p]

        @pl.loop(row, row + row_count)
        def _(i):
            for k in range(n_chip - 1):
                add_slots(i, far_from[k] * 2 + side, False, slot, slot_count)

    for t in range(len(pieces)):
        for k in range(n_chip - 1):
            far_copy(k, t).wait_recv()
            pass_copy(k, t).start()
        if t > 0:
            for k in range(n_chip - 1):
                pass_copy(k, t - 1).wait_recv()
            add_piece(t - 1, 1 - core)
        add_piece(t, core)
    for k in range(n_chip - 1):
        pass_copy(k, len(pieces) - 1).wait_recv()
    add_piece(len(pieces) - 1, 1 - core)

    for way in (0, 1):
        for hop in range(hops[way]):
            b_copy(way, hop).wait_send()

    @pl.loop(0, chunks)
    def _(t):
        near_copy(t).wait_send()

    for t in range(len(pieces)):
        for k in range(n_chip - 1):
            far_copy(k, t).wait_send()
            pass_copy(k, t).wait_send()


def local(n_chip, n_col, a_blocks, a_cols, a_lengths, b_blocks, b_cols, c_cols, order):
    rows, slots, block = a_blocks.shape[0], a_blocks.shape[1], a_blocks.shape[2]
    pattern = c_cols.shape[1]
    panels_each = b_blocks.shape[0]
    panels = panels_each * n_col
    chunk = max(d for d in range(1, max(1, 4 // slots) + 1) if rows % d == 0)
    chunks = rows // chunk
    smem = pl.BlockSpec(memory_space=pltpu.SMEM)
    hbm = pl.BlockSpec(memory_space=pl.ANY)
    dma = pltpu.SemaphoreType.DMA
    return pl.pallas_call(
        functools.partial(kernel, n_chip, n_col, chunk),
        out_shape=pltpu.VMEM((rows, pattern, block, block), jnp.float32),
        in_specs=[smem] * 5 + [hbm] * 2,
        out_specs=pl.BlockSpec(memory_space=pltpu.VMEM),
        scratch_shapes=[
            pltpu.VMEM((n_chip * 2, rows, slots, block, block), jnp.float32),
            pltpu.VMEM((panels, block, block), jnp.float32),
            pltpu.VMEM((panels, 2 * block, 2 * block), jnp.bfloat16),
            dma((2,)),
            dma((chunks,)),
            dma((chunks,)),
            dma((n_chip - 1, len(cut(rows, slots)))),
            dma((n_chip - 1, len(cut(rows, slots)))),
            dma((n_chip - 1, len(cut(rows, slots)))),
            dma((n_chip - 1, len(cut(rows, slots)))),
            dma((2, n_col // 2)),
            dma((2, n_col // 2)),
        ],
        compiler_params=pltpu.CompilerParams(
            collective_id=0, has_side_effects=True, vmem_limit_bytes=60 * 1024 * 1024
        ),
        cost_estimate=pl.CostEstimate(
            flops=2 * rows * slots * 2 * n_chip * 4 * block**3,
            bytes_accessed=4 * rows * block * block * (slots + pattern),
            transcendentals=0,
        ),
    )(a_cols, a_lengths, b_cols.reshape(-1), c_cols.T, order, a_blocks, b_blocks.reshape(panels_each, block, block))


def solution(mesh):
    return jax.shard_map(
        functools.partial(local, mesh.shape["row"] // 2, mesh.shape["col"]),
        mesh=mesh,
        in_specs=(
            P("col", "row", None, None),
            P("col", None),
            P("col"),
            P("col", "row", None, None),
            P(None, "row"),
            P("col", "row"),
            P(),
        ),
        out_specs=P("col", "row", None, None),
        check_vma=False,
    )
```

```python
import functools

import jax
import jax.numpy as jnp
from jax import lax
from jax.experimental import pallas as pl
from jax.experimental.pallas import tpu as pltpu
from jax.sharding import PartitionSpec as P

MESH = pl.DeviceIdType.MESH


def ring_spot(col, n_col):
    odd = col % 2
    return (1 - odd) * (col // 2) + odd * (n_col - 1 - col // 2)


def ring_col(spot, n_col):
    back = spot // (n_col // 2)
    return (1 - back) * (2 * spot) + back * (2 * (n_col - 1 - spot) + 1)


def cut(rows, slots):
    pieces, row = [], 0
    while row < rows - 1:
        size = (rows - 1 - row + 2) // 3
        pieces.append((row, size, 0, slots))
        row += size
    slot = 0
    while slot < slots:
        size = (slots - slot + 1) // 2
        pieces.append((row, 1, slot, size))
        slot += size
    return pieces


def kernel(
    n_chip, n_col, chunk, a_cols, a_lengths, b_cols, c_cols, order, a_ref, b_ref, acc,
    a_all, b_all, b_split,
    own_sem, near_send, near_recv, far_send, far_recv, pass_send, pass_recv, b_send, b_recv,
):
    rows, slots, block = a_ref.shape[0], a_ref.shape[1], a_ref.shape[2]
    pattern = c_cols.shape[0]
    panels_each = b_ref.shape[0]
    panels = b_all.shape[0]
    chunks = rows // chunk
    me, my_col = lax.axis_index("row"), lax.axis_index("col")
    chip, core = me // 2, me % 2
    sibling = chip * 2 + 1 - core
    far = [lax.rem(chip + step, n_chip) * 2 + core for step in range(1, n_chip)]
    far_from = [lax.rem(chip + n_chip - step, n_chip) for step in range(1, n_chip)]
    spot = ring_spot(my_col, n_col)
    ring = [ring_col(lax.rem(spot + step, n_col), n_col) for step in (1, n_col - 1)]
    hops = (n_col // 2, (n_col - 1) // 2)

    barrier = pltpu.get_barrier_semaphore()
    for peer in [sibling] + far:
        pl.semaphore_signal(barrier, inc=1, device_id={"row": peer}, device_id_type=MESH)
    for peer in ring:
        pl.semaphore_signal(barrier, inc=1, device_id={"col": peer}, device_id_type=MESH)
    pl.semaphore_wait(barrier, n_chip + 2)

    def part(t):
        return pl.ds(t * chunk, chunk)

    def own_copy():
        return pltpu.make_async_copy(a_ref, a_all.at[me], own_sem.at[0])

    def own_b():
        return pltpu.make_async_copy(b_ref, b_all.at[pl.ds(my_col * panels_each, panels_each)], own_sem.at[1])

    def near_copy(t):
        return pltpu.make_async_remote_copy(
            src_ref=a_all.at[me, part(t)], dst_ref=a_all.at[me, part(t)],
            send_sem=near_send.at[t], recv_sem=near_recv.at[t],
            device_id={"row": sibling}, device_id_type=MESH,
        )

    pieces = cut(rows, slots)

    def piece(p):
        row, row_count, slot, slot_count = pieces[p]
        return pl.ds(row, row_count), pl.ds(slot, slot_count)

    def far_copy(k, t):
        return pltpu.make_async_remote_copy(
            src_ref=a_ref.at[piece(t)] if t == 0 else a_all.at[(me,) + piece(t)], dst_ref=a_all.at[(me,) + piece(t)],
            send_sem=far_send.at[k, t], recv_sem=far_recv.at[k, t],
            device_id={"row": far[k]}, device_id_type=MESH,
        )

    def pass_copy(k, t):
        source = far_from[k] * 2 + core
        return pltpu.make_async_remote_copy(
            src_ref=a_all.at[(source,) + piece(t)], dst_ref=a_all.at[(source,) + piece(t)],
            send_sem=pass_send.at[k, t], recv_sem=pass_recv.at[k, t],
            device_id={"row": sibling}, device_id_type=MESH,
        )

    def b_copy(way, hop):
        back = hop if way == 1 else n_col - hop
        here = pl.ds(ring_col(lax.rem(spot + back, n_col), n_col) * panels_each, panels_each)
        return pltpu.make_async_remote_copy(
            src_ref=b_all.at[here], dst_ref=b_all.at[here],
            send_sem=b_send.at[way, hop], recv_sem=b_recv.at[way, hop],
            device_id={"col": ring[way]}, device_id_type=MESH,
        )

    own_b().start()

    own_copy().start()
    for k in range(n_chip - 1):
        far_copy(k, 0).start()
    own_b().wait()
    for way in (0, 1):
        b_copy(way, 0).start()
    own_copy().wait()
    for t in range(1, len(pieces)):
        for k in range(n_chip - 1):
            far_copy(k, t).start()

    @pl.loop(0, chunks)
    def _(t):
        near_copy(t).start()

    for way in (0, 1):
        b_copy(way, 0).wait_recv()
    for hop in range(1, hops[0]):
        for way in (0, 1):
            if hop < hops[way]:
                b_copy(way, hop).start()
        for way in (0, 1):
            if hop < hops[way]:
                b_copy(way, hop).wait_recv()

    @pl.loop(0, panels)
    def _(p):
        whole = b_all[p]
        high = whole.astype(jnp.bfloat16)
        low = (whole - high.astype(jnp.float32)).astype(jnp.bfloat16)
        both = jnp.concatenate([high, low], axis=1)
        b_split[p, :block, :] = both
        b_split[p, block:, :] = both

    def add_slots(i, source, first, start=0, count=slots):
        products, marks = [], []
        for j in range(start, start + count):
            slot = source * slots + j
            whole = a_all[source, i, j]
            high = whole.astype(jnp.bfloat16)
            low = (whole - high.astype(jnp.float32)).astype(jnp.bfloat16)
            position = order[a_cols[i, slot]]
            window = b_cols[position]
            live = slot < a_lengths[i]
            marks.append([
                jnp.where(jnp.logical_and(live, window == c_cols[s, i]), 1.0, 0.0).astype(jnp.float32)
                for s in range(pattern)
            ])
            wide = jnp.dot(
                jnp.concatenate([high, low], axis=1), b_split[position],
                preferred_element_type=jnp.float32,
            )
            products.append(wide[:, :block] + wide[:, block:])
        for s in range(pattern):
            total = marks[0][s] * products[0]
            for j in range(1, count):
                total += marks[j][s] * products[j]
            if first:
                acc[i, s] = total
            else:
                acc[i, s] += total

    @pl.loop(0, chunks)
    def _(t):
        near_copy(t).wait_recv()

        @pl.loop(t * chunk, (t + 1) * chunk)
        def _(i):
            add_slots(i, me, True)
            add_slots(i, sibling, False)

    def add_piece(p, side):
        row, row_count, slot, slot_count = pieces[p]

        @pl.loop(row, row + row_count)
        def _(i):
            for k in range(n_chip - 1):
                add_slots(i, far_from[k] * 2 + side, False, slot, slot_count)

    for t in range(len(pieces)):
        for k in range(n_chip - 1):
            far_copy(k, t).wait_recv()
            pass_copy(k, t).start()
        if t > 0:
            for k in range(n_chip - 1):
                pass_copy(k, t - 1).wait_recv()
            add_piece(t - 1, 1 - core)
        add_piece(t, core)
    for k in range(n_chip - 1):
        pass_copy(k, len(pieces) - 1).wait_recv()
    add_piece(len(pieces) - 1, 1 - core)

    for way in (0, 1):
        for hop in range(hops[way]):
            b_copy(way, hop).wait_send()

    @pl.loop(0, chunks)
    def _(t):
        near_copy(t).wait_send()

    for t in range(len(pieces)):
        for k in range(n_chip - 1):
            far_copy(k, t).wait_send()
            pass_copy(k, t).wait_send()


def write_kernel(sums, out_ref, sem):
    rows = sums.shape[0]
    copies = [pltpu.make_async_copy(sums.at[i], out_ref.at[i], sem.at[i]) for i in range(rows)]
    for copy in copies:
        copy.start()
    for copy in copies:
        copy.wait()


def local(n_chip, n_col, a_blocks, a_cols, a_lengths, b_blocks, b_cols, c_cols, order):
    rows, slots, block = a_blocks.shape[0], a_blocks.shape[1], a_blocks.shape[2]
    pattern = c_cols.shape[1]
    panels_each = b_blocks.shape[0]
    panels = panels_each * n_col
    chunk = max(d for d in range(1, max(1, 4 // slots) + 1) if rows % d == 0)
    chunks = rows // chunk
    smem = pl.BlockSpec(memory_space=pltpu.SMEM)
    hbm = pl.BlockSpec(memory_space=pl.ANY)
    dma = pltpu.SemaphoreType.DMA
    sums = pl.pallas_call(
        functools.partial(kernel, n_chip, n_col, chunk),
        out_shape=pltpu.VMEM((rows, pattern, block, block), jnp.float32),
        in_specs=[smem] * 5 + [hbm] * 2,
        out_specs=pl.BlockSpec(memory_space=pltpu.VMEM),
        scratch_shapes=[
            pltpu.VMEM((n_chip * 2, rows, slots, block, block), jnp.float32),
            pltpu.VMEM((panels, block, block), jnp.float32),
            pltpu.VMEM((panels, 2 * block, 2 * block), jnp.bfloat16),
            dma((2,)),
            dma((chunks,)),
            dma((chunks,)),
            dma((n_chip - 1, len(cut(rows, slots)))),
            dma((n_chip - 1, len(cut(rows, slots)))),
            dma((n_chip - 1, len(cut(rows, slots)))),
            dma((n_chip - 1, len(cut(rows, slots)))),
            dma((2, n_col // 2)),
            dma((2, n_col // 2)),
        ],
        compiler_params=pltpu.CompilerParams(
            collective_id=0, has_side_effects=True, vmem_limit_bytes=60 * 1024 * 1024
        ),
        cost_estimate=pl.CostEstimate(
            flops=2 * rows * slots * 2 * n_chip * 4 * block**3,
            bytes_accessed=4 * rows * block * block * (slots + pattern),
            transcendentals=0,
        ),
    )(a_cols, a_lengths, b_cols.reshape(-1), c_cols.T, order, a_blocks, b_blocks.reshape(panels_each, block, block))
    return pl.pallas_call(
        write_kernel,
        out_shape=jax.ShapeDtypeStruct(sums.shape, sums.dtype),
        in_specs=[pl.BlockSpec(memory_space=pltpu.VMEM)],
        out_specs=hbm,
        scratch_shapes=[dma((rows,))],
        compiler_params=pltpu.CompilerParams(vmem_limit_bytes=60 * 1024 * 1024),
    )(pltpu.with_memory_space_constraint(sums, pltpu.VMEM))


def solution(mesh):
    return jax.shard_map(
        functools.partial(local, mesh.shape["row"] // 2, mesh.shape["col"]),
        mesh=mesh,
        in_specs=(
            P("col", "row", None, None),
            P("col", None),
            P("col"),
            P("col", "row", None, None),
            P(None, "row"),
            P("col", "row"),
            P(),
        ),
        out_specs=P("col", "row", None, None),
        check_vma=False,
    )
```
